32 devices in a mesh: ctx: 4 (over y, core), ch: 8 (over z, x).
Axes of the slice: x: 2, y: 2, z: 4, core: 2. Of those that a mesh axis runs over, the one named last changes fastest.
Arguments:
- cotangent: bfloat16 [2048, 4096], P('ctx'), may hold values from -6 to 6
- out_weight: bfloat16 [4096, 4096], P('ch'), may hold values from -0.09375 to 0.09375
- gate_act: bfloat16 [4096, 2048], P('ch', 'ctx'), may hold values from -6 to 6
- conv_input: bfloat16 [4096, 2048], P('ch', 'ctx'), may hold values from -6 to 6
- conv_output: bfloat16 [4096, 2048], P('ch', 'ctx'), may hold values from -6 to 6
- filters: float32 [4096, 128], P('ch'), may hold values from -0.5 to 0.5
- dilation: int32 [8], P('ch'), may hold values from 1 to 64, as said below
- segment_ids: int32 [2048], replicated, may hold values from 0 to 3, never falling along the last dimension, each value on 1 to 1024 neighbouring positions
Outputs:
- grad_gate: bfloat16 [4096, 2048], P('ch', 'ctx')
- grad_input: bfloat16 [4096, 2048], P('ch', 'ctx')
- grad_filter: float32 [4096, 128], P('ch')
The draws below stay inside these ranges and needn't reach their ends.
Inputs may be any that keep to these rules, and one draw needn't show every extreme that they name: `dilation`: every entry is a power of two, and some group has 64.
All inputs are finite; a program needn't handle non-finite values.
Results may differ from the reference program's by a relative error of at most 0.0049.
Values may be sent and summed in bfloat16 or wider, within the bound.
A program may use at most 64 MiB of HBM per device.

```python
import math
import jax
import jax.numpy as jnp
import numpy as np
from jax import lax

D = 4096
KT = 128
MAXDIL = 64
NDOCS = 4
TOKENS = 2048
LEVELS = 8


def draw_dilation(key, part):
    key_power = jax.random.fold_in(key, 11)
    key_level = jax.random.fold_in(key, 12)
    powers = jax.random.randint(key_power, (LEVELS,), 0, 7)
    chosen = jax.random.randint(key_level, (), 0, LEVELS)
    powers = jnp.where(jnp.arange(LEVELS) == chosen, 6, powers)
    return (2 ** powers).astype(jnp.int32)


def shard_levels(key, extent, pieces, least, high):
    loudness, own = 1.0, jax.random.fold_in(key, 6)
    for axis_at, parts in pieces:
        steps = jnp.exp(jax.random.uniform(jax.random.fold_in(own, axis_at), (parts,), jnp.float32, least / len(pieces), high / len(pieces)))
        loudness = loudness * jnp.repeat(steps, extent[axis_at] // parts).reshape([-1 if axis == axis_at else 1 for axis in range(len(extent))])
    return loudness


def split_up(number_of, total, most, skew):
    weights = [(1 << 20) // math.isqrt(rank ** skew) + 1 for rank in range(2, number_of + 1)]
    rest, counts = total - most - (number_of - 1), [1] * (number_of - 1)
    while rest > 0:
        candidates = [i for i in range(number_of - 1) if counts[i] < most]
        pool, budget = sum([weights[i] for i in candidates]), rest
        for i in candidates:
            more = min(most - counts[i], max(1, budget * weights[i] // pool), rest)
            counts[i] = counts[i] + more
            rest = rest - more
    return np.array([most] + counts)


def uneven_parts(key, amount, total, limit, lean):
    if amount == 2:
        one = jax.random.randint(key, (), max(1, total - limit), min(limit, total - 1) + 1)
        return jnp.stack([one, total - one])
    sizes = jnp.asarray(split_up(amount, total, limit, lean), jnp.int32)
    twos = (amount - 1) // 2
    giver, sink = sizes[1:1 + 2 * twos:2], sizes[2:2 + 2 * twos:2]
    room = jnp.minimum(giver - 1, limit - sink)
    passed = jax.random.randint(jax.random.fold_in(key, 1), (twos,), 0, 1 << 20) % (room + 1)
    sizes = sizes.at[1:1 + 2 * twos:2].set(giver - passed).at[2:2 + 2 * twos:2].set(sink + passed)
    return sizes[jax.random.permutation(jax.random.fold_in(key, 2), amount)]


def normal_values(rng, extent, deviation, limit, shards=(), kind=jnp.bfloat16):
    drawn = deviation * jax.random.normal(rng, extent, jnp.float32)
    if shards:
        drawn = drawn * shard_levels(rng, extent, shards, -0.22, 0.18)
    return jnp.clip(drawn, -limit, limit).astype(kind)


def setup_inputs(seed: int = 0) -> dict:
    streams_of = jax.random.split(jax.random.key(seed), 9)
    return {
        "cotangent": normal_values(streams_of[0], (TOKENS, D), 1.0, 6.0, ((0, 4),)),
        "out_weight": normal_values(streams_of[1], (D, D), D ** -0.5, 0.09375, ((0, 8),)),
        "gate_act": normal_values(streams_of[2], (D, TOKENS), 1.0, 6.0, ((0, 8), (1, 4))),
        "conv_input": normal_values(streams_of[3], (D, TOKENS), 1.0, 6.0, ((0, 8), (1, 4))),
        "conv_output": normal_values(streams_of[4], (D, TOKENS), 1.0, 6.0, ((0, 8), (1, 4))),
        "filters": normal_values(streams_of[5], (D, KT), KT ** -0.5, 0.5, ((0, 8),), jnp.float32),
        "dilation": draw_dilation(jax.random.fold_in(streams_of[8], 71), 0),
        "segment_ids": jnp.searchsorted(jnp.cumsum(uneven_parts(streams_of[7], NDOCS, TOKENS, TOKENS // 2, 0)), jnp.arange(TOKENS), side="right").astype(jnp.int32),
    }


def reference(cotangent, out_weight, gate_act, conv_input, conv_output, filters, dilation, segment_ids):
    grad_mix = jnp.dot(out_weight, cotangent.T, preferred_element_type=jnp.float32)
    grad_gate = (grad_mix * conv_output.astype(jnp.float32)).astype(jnp.bfloat16)
    carried = (grad_mix * gate_act.astype(jnp.float32)).astype(jnp.bfloat16)
    reach = MAXDIL * (KT - 1)
    carried_pad = jnp.concatenate([carried, jnp.zeros((D, reach), jnp.bfloat16)], axis=1)
    seg_pad = jnp.concatenate([segment_ids, jnp.full((reach,), -1, jnp.int32)])
    group = D // LEVELS

    def one_level(level):
        start = (level * group).astype(jnp.int32)
        rows_here = lax.dynamic_slice_in_dim(carried_pad, start, group, 0)
        inputs = lax.dynamic_slice_in_dim(conv_input, start, group, 0).astype(jnp.float32)
        taps = lax.dynamic_slice_in_dim(filters, start, group, 0)
        span = dilation[level]

        def tap_step(tap_index, state):
            total, columns = state
            tap_index = jnp.asarray(tap_index).astype(jnp.int32)
            offset = (span * tap_index).astype(jnp.int32)
            slab = lax.dynamic_slice_in_dim(rows_here, offset, TOKENS, 1).astype(jnp.float32)
            keep = lax.dynamic_slice_in_dim(seg_pad, offset, TOKENS, 0) == segment_ids
            term = jnp.where(keep[None, :], slab, jnp.float32(0.0))
            total = total + lax.dynamic_slice_in_dim(taps, tap_index, 1, 1) * term
            column = lax.optimization_barrier(jnp.sum(inputs * term, axis=1))[:, None]
            columns = lax.dynamic_update_slice_in_dim(columns, column, tap_index, 1)
            return (total, columns)
        total, columns = lax.fori_loop(0, KT, tap_step, (jnp.zeros((group, TOKENS), jnp.float32), jnp.zeros((group, KT), jnp.float32)))
        return (total.astype(jnp.bfloat16), columns)
    grad_levels, filter_levels = lax.map(one_level, jnp.arange(LEVELS, dtype=jnp.int32))
    grad_input = grad_levels.reshape(D, TOKENS)
    grad_filter = filter_levels.reshape(D, KT) * (1.0 / math.sqrt(TOKENS))
    return (grad_gate, grad_input, grad_filter)
```

```python
import math

import jax
import jax.numpy as jnp
from jax import lax
from jax.experimental import pallas as pl
from jax.experimental.pallas import tpu as pltpu
from jax.sharding import PartitionSpec as P

KT = 128
MAXDIL = 64
NDOCS = 4
TB = 8
JB = 8
LANES = 128
SUB = 16
SLICE = 2048


def tree(values):
    while len(values) > 1:
        values = [a + b for a, b in zip(values[::2], values[1::2])]
    return values[0]


def conv_kernel(scal_ref, x_ref, u_ref, r_ref, f_ref, total_ref, cols_ref):
    length = u_ref.shape[0]
    blocks = length // TB
    span = scal_ref[0]
    total_ref[...] = jnp.zeros_like(total_ref)
    cols_ref[...] = jnp.zeros_like(cols_ref)

    def token_block(tb, _):
        t0 = tb * TB
        fast = scal_ref[1 + tb]
        last = scal_ref[1 + blocks + tb]

        def tile(jb, masked):
            j0 = jb * JB
            u = [u_ref[t0 + i] for i in range(TB)]
            products = [[] for _ in range(TB)]
            for inner in range(JB):
                tap = j0 + inner
                base = t0 + span * tap
                x = [x_ref[base + i] for i in range(TB)]
                if masked:
                    at = jnp.full((SUB, LANES), tap.astype(jnp.float32)).astype(jnp.bfloat16)
                    x = [jnp.where(r_ref[t0 + i] > at, x[i], jnp.zeros_like(x[i])) for i in range(TB)]
                f = f_ref[tap]
                for i in range(TB):
                    products[i].append(f * x[i])
                cols_ref[tap] += tree([u[i] * x[i] for i in range(TB)]).astype(jnp.float32)
            for i in range(TB):
                total_ref[t0 + i] += tree(products[i]).astype(jnp.float32)
            return None

        def fast_step(jb, c):
            tile(jb, False)
            return c

        def slow_step(jb, c):
            tile(jb, True)
            return c

        lax.fori_loop(0, fast, fast_step, 0)
        lax.fori_loop(fast, last, slow_step, 0)
        return 0

    lax.fori_loop(0, blocks, token_block, 0)


def shifted(block, axis, distance):
    devices = range(lax.axis_size(axis))
    route = [(i - distance, i) for i in devices if i - distance in devices]
    return lax.ppermute(block, axis, route)


def on_device(
    cotangent, out_weight, gate_act, conv_input, conv_output, filters, dilation, segment_ids
):
    channels, rows = gate_act.shape
    ctx_count = lax.axis_size("ctx")
    position = lax.axis_index("ctx")
    tokens = rows * ctx_count
    longest = tokens // 2
    groups = channels // LANES
    streams = SUB // groups
    length = rows // streams
    reach = min(MAXDIL * KT, longest)
    depth = min(ctx_count - 1, (reach + rows - 1) // rows)

    grad_mix = lax.dot_general(
        out_weight, cotangent, (((1,), (1,)), ((), ())), preferred_element_type=jnp.float32
    )
    grad_gate = (grad_mix * conv_output.astype(jnp.float32)).astype(jnp.bfloat16)
    carried = (grad_mix * gate_act.astype(jnp.float32)).astype(jnp.bfloat16)
    turned = carried.T
    pieces = [turned] + [shifted(turned, "ctx", -k) for k in range(1, depth + 1)]
    extended = jnp.concatenate(pieces, axis=0)
    need = rows + reach
    if extended.shape[0] < need:
        extended = jnp.pad(extended, ((0, need - extended.shape[0]), (0, 0)))
    u4 = conv_input.T.reshape(streams, length, groups, LANES).transpose(1, 0, 2, 3)
    u4 = u4.reshape(length, SUB, LANES)
    f4 = filters.T.astype(jnp.bfloat16).reshape(KT, 1, groups, LANES)
    f4 = jnp.broadcast_to(f4, (KT, streams, groups, LANES)).reshape(KT, SUB, LANES)

    span = dilation[0]
    ends = jnp.sum(
        (segment_ids[None, :] <= jnp.arange(NDOCS, dtype=jnp.int32)[:, None]).astype(jnp.int32), axis=1
    )
    mine = lax.dynamic_slice_in_dim(segment_ids, position * rows, rows, 0)
    end = jnp.zeros((rows,), jnp.int32)
    for doc in range(NDOCS):
        end = jnp.where(mine == doc, ends[doc], end)
    at = position * rows + jnp.arange(rows, dtype=jnp.int32)
    room = jnp.minimum((end - at + span - 1) // span, KT).reshape(streams, length)
    per = room.reshape(streams, length // TB, TB)
    fast = jnp.min(per, axis=(0, 2)) // JB
    last = (jnp.max(per, axis=(0, 2)) + JB - 1) // JB
    parts = max(1, reach // SLICE)
    taps = KT // parts
    window = length + min(reach, MAXDIL * taps)
    whole = pl.BlockSpec(memory_space=pltpu.VMEM)
    call = pl.pallas_call(
        conv_kernel,
        out_shape=(
            jax.ShapeDtypeStruct((length, SUB, LANES), jnp.float32),
            jax.ShapeDtypeStruct((taps, SUB, LANES), jnp.float32),
        ),
        in_specs=[pl.BlockSpec(memory_space=pltpu.SMEM)] + [whole] * 4,
        out_specs=(whole, whole),
        compiler_params=pltpu.CompilerParams(vmem_limit_bytes=40 * 1024 * 1024),
    )

    def run_part(part):
        first = part * taps
        here = extended
        if parts > 1:
            here = lax.dynamic_slice_in_dim(extended, span * first, window + rows - length, 0)
        x4 = jnp.stack([here[k * length : k * length + window] for k in range(streams)], axis=1)
        x4 = x4.reshape(window, SUB, LANES)
        begin = jnp.clip(fast - first // JB, 0, taps // JB)
        stop = jnp.clip(last - first // JB, 0, taps // JB)
        scal = jnp.concatenate([span[None], begin, stop]).astype(jnp.int32)
        left = jnp.maximum(room - first, 0).T.astype(jnp.bfloat16)
        r4 = jnp.broadcast_to(left[:, :, None, None], (length, streams, groups, LANES))
        r4 = r4.reshape(length, SUB, LANES)
        return call(scal, x4, u4, r4, lax.dynamic_slice_in_dim(f4, first, taps, 0))

    if parts == 1:
        total, cols = run_part(0)
    else:

        def part_step(total, part):
            more, cols = run_part(part)
            return total + more, jnp.sum(cols.reshape(taps, streams, channels), axis=1)

        start = jnp.zeros((length, SUB, LANES), jnp.float32)
        total, cols = lax.scan(part_step, start, jnp.arange(parts, dtype=jnp.int32))

    grad_input = total.astype(jnp.bfloat16).reshape(length, streams, channels)
    grad_input = grad_input.transpose(2, 1, 0).reshape(channels, rows)
    cols = jnp.sum(cols.reshape(KT, -1, channels), axis=1)
    grad_filter = lax.psum(cols.T, "ctx") * (1.0 / math.sqrt(tokens))
    return (grad_gate, grad_input, grad_filter)


def solution(mesh):
    in_specs = (
        P("ctx", None),
        P("ch", None),
        P("ch", "ctx"),
        P("ch", "ctx"),
        P("ch", "ctx"),
        P("ch", None),
        P("ch"),
        P(),
    )
    out_specs = (P("ch", "ctx"), P("ch", "ctx"), P("ch", None))
    return jax.shard_map(
        on_device, mesh=mesh, in_specs=in_specs, out_specs=out_specs, check_vma=False
    )
```

```python
import functools
import math

import jax
import jax.numpy as jnp
from jax import lax
from jax.experimental import pallas as pl
from jax.experimental.pallas import tpu as pltpu
from jax.sharding import PartitionSpec as P

KT = 128
MAXDIL = 64
NDOCS = 4
TB = 8
JB = 8
LANES = 128
SUB = 16


def tree(values):
    while len(values) > 1:
        values = [a + b for a, b in zip(values[::2], values[1::2])]
    return values[0]


def conv_kernel(
    scal_ref, ext_ref, in_ref, r_ref, f_ref, gi_ref, gf_ref,
    wide_ref, side_ref, x_ref, u_ref, f4_ref, total_ref, cols_ref, *, scale
):
    groups, length = u_ref.shape[:2]
    blocks = length // TB
    span = scal_ref[0]
    built = scal_ref[1]
    total_ref[...] = jnp.zeros_like(total_ref)
    cols_ref[...] = jnp.zeros_like(cols_ref)
    for g in range(groups):
        lanes = slice(g * LANES, (g + 1) * LANES)
        wide_ref[g] = ext_ref[:, lanes].astype(jnp.float32)
        side_ref[g] = in_ref[lanes, :].astype(jnp.float32).T

    def build_filters(tb, _):
        for g in range(groups):
            rows8 = f_ref[pl.ds(pl.multiple_of(tb * 8, 8), 8), g * LANES : (g + 1) * LANES]
            for i in range(8):
                f4_ref[g, tb * 8 + i] = jnp.broadcast_to(rows8[i : i + 1], (SUB, LANES)).astype(jnp.bfloat16)
        return 0

    lax.fori_loop(0, KT // 8, build_filters, 0)

    def build_inputs(tb, _):
        for g in range(groups):
            for i in range(TB):
                t = tb * TB + i
                u_ref[g, t] = side_ref[g, pl.ds(t, SUB, stride=length), :].astype(jnp.bfloat16)
        return 0

    lax.fori_loop(0, blocks, build_inputs, 0)

    def build_window(tb, _):
        for g in range(groups):
            for i in range(TB):
                t = tb * TB + i
                x_ref[g, t] = wide_ref[g, pl.ds(t, SUB, stride=length), :].astype(jnp.bfloat16)
        return 0

    lax.fori_loop(0, built, build_window, 0)

    def token_block(tb, _):
        t0 = tb * TB
        fast = scal_ref[2 + tb]
        last = scal_ref[2 + blocks + tb]

        def tile(jb, masked):
            j0 = jb * JB
            if masked:
                keep = []
                zero = jnp.zeros((SUB, LANES), jnp.bfloat16)
                one = jnp.ones((SUB, LANES), jnp.bfloat16)
                for inner in range(JB):
                    at = jnp.full((SUB, LANES), (j0 + inner).astype(jnp.float32)).astype(jnp.bfloat16)
                    keep.append(
                        [jnp.minimum(jnp.maximum(r_ref[t0 + i] - at, zero), one) for i in range(TB)]
                    )
            for g in range(groups):
                u = [u_ref[g, t0 + i] for i in range(TB)]
                products = [[] for _ in range(TB)]
                for inner in range(JB):
                    tap = j0 + inner
                    base = t0 + span * tap
                    x = [x_ref[g, base + i] for i in range(TB)]
                    if masked:
                        x = [a * m for a, m in zip(x, keep[inner])]
                    f = f4_ref[g, tap]
                    for i in range(TB):
                        products[i].append(f * x[i])
                    cols_ref[g, tap] += tree([u[i] * x[i] for i in range(TB)]).astype(jnp.float32)
                for i in range(TB):
                    total_ref[g, t0 + i] += tree(products[i]).astype(jnp.float32)

        def fast_step(jb, c):
            tile(jb, False)
            return c

        def slow_step(jb, c):
            tile(jb, True)
            return c

        lax.fori_loop(0, fast, fast_step, 0)
        lax.fori_loop(fast, last, slow_step, 0)
        for g in range(groups):
            for i in range(TB):
                side_ref[g, pl.ds(t0 + i, SUB, stride=length), :] = total_ref[g, t0 + i]
        return 0

    lax.fori_loop(0, blocks, token_block, 0)
    for g in range(groups):
        lanes = slice(g * LANES, (g + 1) * LANES)
        gi_ref[lanes, :] = side_ref[g].T.astype(jnp.bfloat16)
        gf_ref[lanes, :] = jnp.sum(cols_ref[g], axis=1).T * scale


def shifted(block, axis, distance):
    devices = range(lax.axis_size(axis))
    route = [(i - distance, i) for i in devices if i - distance in devices]
    return lax.ppermute(block, axis, route)


def on_device(
    cotangent, out_weight, gate_act, conv_input, conv_output, filters, dilation, segment_ids
):
    channels, rows = gate_act.shape
    ctx_count = lax.axis_size("ctx")
    position = lax.axis_index("ctx")
    tokens = rows * ctx_count
    longest = tokens // 2
    groups = channels // LANES
    length = rows // SUB
    reach = min(MAXDIL * KT, longest)
    depth = min(ctx_count - 1, (reach + rows - 1) // rows)

    grad_mix = lax.dot_general(
        out_weight, cotangent, (((1,), (1,)), ((), ())), preferred_element_type=jnp.float32
    )
    grad_gate = (grad_mix * conv_output.astype(jnp.float32)).astype(jnp.bfloat16)
    carried = (grad_mix * gate_act.astype(jnp.float32)).astype(jnp.bfloat16)
    turned = carried.T
    pieces = [turned] + [shifted(turned, "ctx", -k) for k in range(1, depth + 1)]
    extended = jnp.concatenate(pieces, axis=0)
    need = rows + reach
    extended = extended[:need]
    if extended.shape[0] < need:
        extended = jnp.pad(extended, ((0, need - extended.shape[0]), (0, 0)))
    span = dilation[0]
    ends = jnp.sum(
        (segment_ids[None, :] <= jnp.arange(NDOCS, dtype=jnp.int32)[:, None]).astype(jnp.int32), axis=1
    )
    mine = lax.dynamic_slice_in_dim(segment_ids, position * rows, rows, 0)
    end = jnp.zeros((rows,), jnp.int32)
    for doc in range(NDOCS):
        end = jnp.where(mine == doc, ends[doc], end)
    at = position * rows + jnp.arange(rows, dtype=jnp.int32)
    room = jnp.minimum((end - at + span - 1) // span, KT).reshape(SUB, length)
    per = room.reshape(SUB, length // TB, TB)
    fast = jnp.min(per, axis=(0, 2)) // JB
    last = (jnp.max(per, axis=(0, 2)) + JB - 1) // JB
    built = jnp.minimum(length + span * JB * jnp.max(last), length + reach) // TB
    scal = jnp.concatenate([span[None], built[None], fast, last]).astype(jnp.int32)
    r4 = jnp.broadcast_to(room.T.astype(jnp.bfloat16)[:, :, None], (length, SUB, LANES))

    whole = pl.BlockSpec(memory_space=pltpu.VMEM)
    f32, bf16 = jnp.float32, jnp.bfloat16
    grad_input, cols = pl.pallas_call(
        functools.partial(conv_kernel, scale=1.0 / math.sqrt(tokens)),
        out_shape=(
            jax.ShapeDtypeStruct((channels, rows), bf16),
            jax.ShapeDtypeStruct((channels, KT), f32),
        ),
        in_specs=[pl.BlockSpec(memory_space=pltpu.SMEM)] + [whole] * 4,
        out_specs=(whole, whole),
        scratch_shapes=[
            pltpu.VMEM((groups, need, LANES), f32),
            pltpu.VMEM((groups, rows, LANES), f32),
            pltpu.VMEM((groups, length + reach, SUB, LANES), bf16),
            pltpu.VMEM((groups, length, SUB, LANES), bf16),
            pltpu.VMEM((groups, KT, SUB, LANES), bf16),
            pltpu.VMEM((groups, length, SUB, LANES), f32),
            pltpu.VMEM((groups, KT, SUB, LANES), f32),
        ],
        compiler_params=pltpu.CompilerParams(vmem_limit_bytes=56 * 1024 * 1024),
    )(scal, extended, conv_input, r4, filters.T)

    step = 1
    while step < ctx_count:
        route = [(i, i ^ step) for i in range(ctx_count)]
        cols = cols + lax.ppermute(cols, "ctx", route)
        step *= 2
    return (grad_gate, grad_input, cols)


def solution(mesh):
    in_specs = (
        P("ctx", None),
        P("ch", None),
        P("ch", "ctx"),
        P("ch", "ctx"),
        P("ch", "ctx"),
        P("ch", None),
        P("ch"),
        P(),
    )
    out_specs = (P("ch", "ctx"), P("ch", "ctx"), P("ch", None))
    return jax.shard_map(
        on_device, mesh=mesh, in_specs=in_specs, out_specs=out_specs, check_vma=False
    )
```

```python
import functools
import math

import jax
import jax.numpy as jnp
from jax import lax
from jax.experimental import pallas as pl
from jax.experimental.pallas import tpu as pltpu
from jax.sharding import PartitionSpec as P

KT = 128
MAXDIL = 64
NDOCS = 4
TB = 8
JB = 8
LANES = 128
SUB = 16


def tree(values):
    while len(values) > 1:
        values = [a + b for a, b in zip(values[::2], values[1::2])]
    return values[0]


def conv_kernel(
    scal_ref, ext_ref, in_ref, r_ref, f_ref, gi_ref, gf_ref,
    wide_ref, base_ref, side_ref, x_ref, u_ref, f4_ref, total_ref, cols_ref, *, scale
):
    groups, length = u_ref.shape[:2]
    blocks = length // TB
    span = scal_ref[0]
    built = scal_ref[1]
    total_ref[...] = jnp.zeros_like(total_ref)
    cols_ref[...] = jnp.zeros_like(cols_ref)
    for g in range(groups):
        lanes = slice(g * LANES, (g + 1) * LANES)
        wide_ref[g] = ext_ref[:, lanes].astype(jnp.float32)
        side_ref[g] = in_ref[lanes, :].astype(jnp.float32).T

    def build_filters(tb, _):
        for g in range(groups):
            rows8 = f_ref[pl.ds(pl.multiple_of(tb * 8, 8), 8), g * LANES : (g + 1) * LANES]
            for i in range(8):
                f4_ref[g, tb * 8 + i] = jnp.broadcast_to(rows8[i : i + 1], (SUB, LANES)).astype(jnp.bfloat16)
        return 0

    lax.fori_loop(0, KT // 8, build_filters, 0)

    def build_inputs(tb, _):
        for g in range(groups):
            for i in range(TB):
                t = tb * TB + i
                u_ref[g, t] = side_ref[g, pl.ds(t, SUB, stride=length), :].astype(jnp.bfloat16)
        return 0

    lax.fori_loop(0, blocks, build_inputs, 0)

    def build_base(tb, _):
        for g in range(groups):
            for i in range(TB):
                t = tb * TB + i
                base_ref[g, t] = wide_ref[g, pl.ds(t, base_ref.shape[2], stride=length), :]
        return 0

    lax.fori_loop(0, blocks, build_base, 0)

    def build_window(tb, _):
        first = lax.div(tb, blocks)
        t0 = lax.rem(tb, blocks) * TB
        for g in range(groups):
            for i in range(TB):
                row = base_ref[g, t0 + i, pl.ds(first, SUB), :]
                x_ref[g, tb * TB + i] = row.astype(jnp.bfloat16)
        return 0

    lax.fori_loop(0, built, build_window, 0)

    def token_block(tb, _):
        t0 = tb * TB
        fast = scal_ref[2 + tb]
        last = scal_ref[2 + blocks + tb]

        def tile(jb, masked):
            j0 = jb * JB
            if masked:
                keep = []
                zero = jnp.zeros((SUB, LANES), jnp.bfloat16)
                one = jnp.ones((SUB, LANES), jnp.bfloat16)
                for inner in range(JB):
                    at = jnp.full((SUB, LANES), (j0 + inner).astype(jnp.float32)).astype(jnp.bfloat16)
                    keep.append(
                        [jnp.minimum(jnp.maximum(r_ref[t0 + i] - at, zero), one) for i in range(TB)]
                    )
            for g in range(groups):
                u = [u_ref[g, t0 + i] for i in range(TB)]
                products = [[] for _ in range(TB)]
                for inner in range(JB):
                    tap = j0 + inner
                    base = t0 + span * tap
                    x = [x_ref[g, base + i] for i in range(TB)]
                    if masked:
                        x = [a * m for a, m in zip(x, keep[inner])]
                    f = f4_ref[g, tap]
                    for i in range(TB):
                        products[i].append(f * x[i])
                    cols_ref[g, tap] += tree([u[i] * x[i] for i in range(TB)]).astype(jnp.float32)
                for i in range(TB):
                    total_ref[g, t0 + i] += tree(products[i]).astype(jnp.float32)

        def fast_step(jb, c):
            tile(jb, False)
            return c

        def slow_step(jb, c):
            tile(jb, True)
            return c

        lax.fori_loop(0, fast, fast_step, 0)
        lax.fori_loop(fast, last, slow_step, 0)
        for g in range(groups):
            for i in range(TB):
                side_ref[g, pl.ds(t0 + i, SUB, stride=length), :] = total_ref[g, t0 + i]
        return 0

    lax.fori_loop(0, blocks, token_block, 0)
    for g in range(groups):
        lanes = slice(g * LANES, (g + 1) * LANES)
        gi_ref[lanes, :] = side_ref[g].T.astype(jnp.bfloat16)
        gf_ref[lanes, :] = jnp.sum(cols_ref[g], axis=1).T * scale


def shifted(block, axis, distance):
    devices = range(lax.axis_size(axis))
    route = [(i - distance, i) for i in devices if i - distance in devices]
    return lax.ppermute(block, axis, route)


def on_device(
    cotangent, out_weight, gate_act, conv_input, conv_output, filters, dilation, segment_ids
):
    channels, rows = gate_act.shape
    ctx_count = lax.axis_size("ctx")
    position = lax.axis_index("ctx")
    tokens = rows * ctx_count
    longest = tokens // 2
    groups = channels // LANES
    length = rows // SUB
    reach = min(MAXDIL * KT, longest)
    depth = min(ctx_count - 1, (reach + rows - 1) // rows)

    grad_mix = lax.dot_general(
        out_weight, cotangent, (((1,), (1,)), ((), ())), preferred_element_type=jnp.float32
    )
    grad_gate = (grad_mix * conv_output.astype(jnp.float32)).astype(jnp.bfloat16)
    carried = (grad_mix * gate_act.astype(jnp.float32)).astype(jnp.bfloat16)
    turned = carried.T
    pieces = [turned] + [shifted(turned, "ctx", -k) for k in range(1, depth + 1)]
    extended = jnp.concatenate(pieces, axis=0)
    need = rows + reach
    extended = extended[:need]
    if extended.shape[0] < need:
        extended = jnp.pad(extended, ((0, need - extended.shape[0]), (0, 0)))
    span = dilation[0]
    ends = jnp.sum(
        (segment_ids[None, :] <= jnp.arange(NDOCS, dtype=jnp.int32)[:, None]).astype(jnp.int32), axis=1
    )
    mine = lax.dynamic_slice_in_dim(segment_ids, position * rows, rows, 0)
    end = jnp.zeros((rows,), jnp.int32)
    for doc in range(NDOCS):
        end = jnp.where(mine == doc, ends[doc], end)
    at = position * rows + jnp.arange(rows, dtype=jnp.int32)
    room = jnp.minimum((end - at + span - 1) // span, KT).reshape(SUB, length)
    per = room.reshape(SUB, length // TB, TB)
    fast = jnp.min(per, axis=(0, 2)) // JB
    last = (jnp.max(per, axis=(0, 2)) + JB - 1) // JB
    built = jnp.minimum(length + span * JB * jnp.max(last), length + reach) // TB
    scal = jnp.concatenate([span[None], built[None], fast, last]).astype(jnp.int32)
    r4 = jnp.broadcast_to(room.T.astype(jnp.bfloat16)[:, :, None], (length, SUB, LANES))

    whole = pl.BlockSpec(memory_space=pltpu.VMEM)
    f32, bf16 = jnp.float32, jnp.bfloat16
    grad_input, cols = pl.pallas_call(
        functools.partial(conv_kernel, scale=1.0 / math.sqrt(tokens)),
        out_shape=(
            jax.ShapeDtypeStruct((channels, rows), bf16),
            jax.ShapeDtypeStruct((channels, KT), f32),
        ),
        in_specs=[pl.BlockSpec(memory_space=pltpu.SMEM)] + [whole] * 4,
        out_specs=(whole, whole),
        scratch_shapes=[
            pltpu.VMEM((groups, need, LANES), f32),
            pltpu.VMEM((groups, length, need // length, LANES), f32),
            pltpu.VMEM((groups, rows, LANES), f32),
            pltpu.VMEM((groups, length + reach, SUB, LANES), bf16),
            pltpu.VMEM((groups, length, SUB, LANES), bf16),
            pltpu.VMEM((groups, KT, SUB, LANES), bf16),
            pltpu.VMEM((groups, length, SUB, LANES), f32),
            pltpu.VMEM((groups, KT, SUB, LANES), f32),
        ],
        compiler_params=pltpu.CompilerParams(vmem_limit_bytes=56 * 1024 * 1024),
    )(scal, extended, conv_input, r4, filters.T)

    step = 1
    while step < ctx_count:
        route = [(i, i ^ step) for i in range(ctx_count)]
        cols = cols + lax.ppermute(cols, "ctx", route)
        step *= 2
    return (grad_gate, grad_input, cols)


def solution(mesh):
    in_specs = (
        P("ctx", None),
        P("ch", None),
        P("ch", "ctx"),
        P("ch", "ctx"),
        P("ch", "ctx"),
        P("ch", None),
        P("ch"),
        P(),
    )
    out_specs = (P("ch", "ctx"), P("ch", "ctx"), P("ch", None))
    return jax.shard_map(
        on_device, mesh=mesh, in_specs=in_specs, out_specs=out_specs, check_vma=False
    )
```

```python
import functools
import math

import jax
import jax.numpy as jnp
from jax import lax
from jax.experimental import pallas as pl
from jax.experimental.pallas import tpu as pltpu
from jax.sharding import PartitionSpec as P

KT = 128
MAXDIL = 64
NDOCS = 4
TB = 8
JB = 8
LANES = 128
SUB = 16


def tree(values):
    while len(values) > 1:
        values = [a + b for a, b in zip(values[::2], values[1::2])]
    return values[0]


def conv_kernel(
    scal_ref, in_ref, r_ref, f_ref, *refs, scale
):
    pieces = refs[:-10]
    gi_ref, gf_ref, wide_ref, base_ref, side_ref, x_ref, u_ref, f4_ref, total_ref, cols_ref = refs[-10:]
    groups, length = u_ref.shape[:2]
    rows = in_ref.shape[1]
    blocks = length // TB
    span = scal_ref[0]
    built = scal_ref[1]
    total_ref[...] = jnp.zeros_like(total_ref)
    cols_ref[...] = jnp.zeros_like(cols_ref)
    for g in range(groups):
        lanes = slice(g * LANES, (g + 1) * LANES)
        for k, piece in enumerate(pieces):
            wide_ref[g, k * rows : (k + 1) * rows] = piece[lanes, :].astype(jnp.float32).T
        if len(pieces) * rows < wide_ref.shape[1]:
            wide_ref[g, len(pieces) * rows :] = jnp.zeros(
                (wide_ref.shape[1] - len(pieces) * rows, LANES), jnp.float32
            )
        side_ref[g] = in_ref[lanes, :].astype(jnp.float32).T

    def build_filters(tb, _):
        for g in range(groups):
            rows8 = f_ref[pl.ds(pl.multiple_of(tb * 8, 8), 8), g * LANES : (g + 1) * LANES]
            for i in range(8):
                f4_ref[g, tb * 8 + i] = jnp.broadcast_to(rows8[i : i + 1], (SUB, LANES)).astype(jnp.bfloat16)
        return 0

    lax.fori_loop(0, KT // 8, build_filters, 0)

    def build_inputs(tb, _):
        for g in range(groups):
            for i in range(TB):
                t = tb * TB + i
                u_ref[g, t] = side_ref[g, pl.ds(t, SUB, stride=length), :].astype(jnp.bfloat16)
        return 0

    lax.fori_loop(0, blocks, build_inputs, 0)

    def build_base(tb, _):
        for g in range(groups):
            for i in range(TB):
                t = tb * TB + i
                base_ref[g, t] = wide_ref[g, pl.ds(t, base_ref.shape[2], stride=length), :]
        return 0

    lax.fori_loop(0, blocks, build_base, 0)

    def build_window(tb, _):
        first = lax.div(tb, blocks)
        t0 = lax.rem(tb, blocks) * TB
        for g in range(groups):
            for i in range(TB):
                row = base_ref[g, t0 + i, pl.ds(first, SUB), :]
                x_ref[g, tb * TB + i] = row.astype(jnp.bfloat16)
        return 0

    lax.fori_loop(0, built, build_window, 0)

    def token_block(tb, _):
        t0 = tb * TB
        fast = scal_ref[2 + tb]
        last = scal_ref[2 + blocks + tb]

        def tile(jb, masked):
            j0 = jb * JB
            if masked:
                keep = []
                zero = jnp.zeros((SUB, LANES), jnp.bfloat16)
                one = jnp.ones((SUB, LANES), jnp.bfloat16)
                for inner in range(JB):
                    at = jnp.full((SUB, LANES), (j0 + inner).astype(jnp.float32)).astype(jnp.bfloat16)
                    keep.append(
                        [jnp.minimum(jnp.maximum(r_ref[t0 + i] - at, zero), one) for i in range(TB)]
                    )
            for g in range(groups):
                u = [u_ref[g, t0 + i] for i in range(TB)]
                products = [[] for _ in range(TB)]
                for inner in range(JB):
                    tap = j0 + inner
                    base = t0 + span * tap
                    x = [x_ref[g, base + i] for i in range(TB)]
                    if masked:
                        x = [a * m for a, m in zip(x, keep[inner])]
                    f = f4_ref[g, tap]
                    for i in range(TB):
                        products[i].append(f * x[i])
                    cols_ref[g, tap] += tree([u[i] * x[i] for i in range(TB)]).astype(jnp.float32)
                for i in range(TB):
                    total_ref[g, t0 + i] += tree(products[i]).astype(jnp.float32)

        def fast_step(jb, c):
            tile(jb, False)
            return c

        def slow_step(jb, c):
            tile(jb, True)
            return c

        lax.fori_loop(0, fast, fast_step, 0)
        lax.fori_loop(fast, last, slow_step, 0)
        for g in range(groups):
            for i in range(TB):
                side_ref[g, pl.ds(t0 + i, SUB, stride=length), :] = total_ref[g, t0 + i]
        return 0

    lax.fori_loop(0, blocks, token_block, 0)
    for g in range(groups):
        lanes = slice(g * LANES, (g + 1) * LANES)
        gi_ref[lanes, :] = side_ref[g].T.astype(jnp.bfloat16)
        gf_ref[lanes, :] = jnp.sum(cols_ref[g], axis=1).T * scale


def shifted(block, axis, distance):
    devices = range(lax.axis_size(axis))
    route = [(i - distance, i) for i in devices if i - distance in devices]
    return lax.ppermute(block, axis, route)


def on_device(
    cotangent, out_weight, gate_act, conv_input, conv_output, filters, dilation, segment_ids
):
    channels, rows = gate_act.shape
    ctx_count = lax.axis_size("ctx")
    position = lax.axis_index("ctx")
    tokens = rows * ctx_count
    longest = tokens // 2
    groups = channels // LANES
    length = rows // SUB
    reach = min(MAXDIL * KT, longest)
    depth = min(ctx_count - 1, (reach + rows - 1) // rows)

    grad_mix = lax.dot_general(
        out_weight, cotangent, (((1,), (1,)), ((), ())), preferred_element_type=jnp.float32
    )
    grad_gate = (grad_mix * conv_output.astype(jnp.float32)).astype(jnp.bfloat16)
    carried = (grad_mix * gate_act.astype(jnp.float32)).astype(jnp.bfloat16)
    pieces = [carried] + [shifted(carried, "ctx", -k) for k in range(1, depth + 1)]
    need = max(rows + reach, rows * (depth + 1))
    span = dilation[0]
    ends = jnp.sum(
        (segment_ids[None, :] <= jnp.arange(NDOCS, dtype=jnp.int32)[:, None]).astype(jnp.int32), axis=1
    )
    mine = lax.dynamic_slice_in_dim(segment_ids, position * rows, rows, 0)
    end = jnp.zeros((rows,), jnp.int32)
    for doc in range(NDOCS):
        end = jnp.where(mine == doc, ends[doc], end)
    at = position * rows + jnp.arange(rows, dtype=jnp.int32)
    room = jnp.minimum((end - at + span - 1) // span, KT).reshape(SUB, length)
    per = room.reshape(SUB, length // TB, TB)
    fast = jnp.min(per, axis=(0, 2)) // JB
    last = (jnp.max(per, axis=(0, 2)) + JB - 1) // JB
    built = jnp.minimum(length + span * JB * jnp.max(last), length + reach) // TB
    scal = jnp.concatenate([span[None], built[None], fast, last]).astype(jnp.int32)
    r4 = jnp.broadcast_to(room.T.astype(jnp.bfloat16)[:, :, None], (length, SUB, LANES))

    whole = pl.BlockSpec(memory_space=pltpu.VMEM)
    f32, bf16 = jnp.float32, jnp.bfloat16
    grad_input, cols = pl.pallas_call(
        functools.partial(conv_kernel, scale=1.0 / math.sqrt(tokens)),
        out_shape=(
            jax.ShapeDtypeStruct((channels, rows), bf16),
            jax.ShapeDtypeStruct((channels, KT), f32),
        ),
        in_specs=[pl.BlockSpec(memory_space=pltpu.SMEM)] + [whole] * (3 + len(pieces)),
        out_specs=(whole, whole),
        scratch_shapes=[
            pltpu.VMEM((groups, need, LANES), f32),
            pltpu.VMEM((groups, length, need // length, LANES), f32),
            pltpu.VMEM((groups, rows, LANES), f32),
            pltpu.VMEM((groups, length + reach, SUB, LANES), bf16),
            pltpu.VMEM((groups, length, SUB, LANES), bf16),
            pltpu.VMEM((groups, KT, SUB, LANES), bf16),
            pltpu.VMEM((groups, length, SUB, LANES), f32),
            pltpu.VMEM((groups, KT, SUB, LANES), f32),
        ],
        compiler_params=pltpu.CompilerParams(vmem_limit_bytes=56 * 1024 * 1024),
    )(scal, conv_input, r4, filters.T, *pieces)

    step = 1
    while step < ctx_count:
        route = [(i, i ^ step) for i in range(ctx_count)]
        cols = cols + lax.ppermute(cols, "ctx", route)
        step *= 2
    return (grad_gate, grad_input, cols)


def solution(mesh):
    in_specs = (
        P("ctx", None),
        P("ch", None),
        P("ch", "ctx"),
        P("ch", "ctx"),
        P("ch", "ctx"),
        P("ch", None),
        P("ch"),
        P(),
    )
    out_specs = (P("ch", "ctx"), P("ch", "ctx"), P("ch", None))
    return jax.shard_map(
        on_device, mesh=mesh, in_specs=in_specs, out_specs=out_specs, check_vma=False
    )
```

```python
import functools
import math

import jax
import jax.numpy as jnp
from jax import lax
from jax.experimental import pallas as pl
from jax.experimental.pallas import tpu as pltpu
from jax.sharding import PartitionSpec as P

KT = 128
MAXDIL = 64
NDOCS = 4
TB = 8
JB = 8
LANES = 128
SUB = 16


def tree(values):
    while len(values) > 1:
        values = [a + b for a, b in zip(values[::2], values[1::2])]
    return values[0]


def conv_kernel(
    scal_ref, in_ref, r_ref, f_ref, *refs, scale
):
    pieces = refs[:-10]
    gi_ref, gf_ref, wide_ref, base_ref, side_ref, x_ref, u_ref, f4_ref, total_ref, cols_ref = refs[-10:]
    groups, length = u_ref.shape[:2]
    rows = in_ref.shape[1]
    blocks = length // TB
    span = scal_ref[0]
    built = scal_ref[1]
    total_ref[...] = jnp.zeros_like(total_ref)
    cols_ref[...] = jnp.zeros_like(cols_ref)
    for g in range(groups):
        lanes = slice(g * LANES, (g + 1) * LANES)
        for k, piece in enumerate(pieces):
            wide_ref[g, k * rows : (k + 1) * rows] = piece[lanes, :].astype(jnp.float32).T
        if len(pieces) * rows < wide_ref.shape[1]:
            wide_ref[g, len(pieces) * rows :] = jnp.zeros(
                (wide_ref.shape[1] - len(pieces) * rows, LANES), jnp.float32
            )
        side_ref[g] = in_ref[lanes, :].astype(jnp.float32).T

    def build_filters(tb, _):
        for g in range(groups):
            rows8 = f_ref[pl.ds(pl.multiple_of(tb * 8, 8), 8), g * LANES : (g + 1) * LANES]
            for i in range(8):
                f4_ref[g, tb * 8 + i] = jnp.broadcast_to(rows8[i : i + 1], (SUB, LANES)).astype(jnp.bfloat16)
        return 0

    lax.fori_loop(0, KT // 8, build_filters, 0)

    def build_inputs(tb, _):
        for g in range(groups):
            for i in range(TB):
                t = tb * TB + i
                u_ref[g, t] = side_ref[g, pl.ds(t, SUB, stride=length), :].astype(jnp.bfloat16)
        return 0

    lax.fori_loop(0, blocks, build_inputs, 0)

    def build_base(tb, _):
        for g in range(groups):
            for i in range(TB):
                t = tb * TB + i
                base_ref[g, t] = wide_ref[g, pl.ds(t, base_ref.shape[2], stride=length), :]
        return 0

    lax.fori_loop(0, blocks, build_base, 0)

    def build_window(tb, _):
        first = lax.div(tb, blocks)
        t0 = lax.rem(tb, blocks) * TB
        for g in range(groups):
            for i in range(TB):
                row = base_ref[g, t0 + i, pl.ds(first, SUB), :]
                x_ref[g, tb * TB + i] = row.astype(jnp.bfloat16)
        return 0

    lax.fori_loop(0, built, build_window, 0)

    def token_block(tb, _):
        t0 = tb * TB
        fast = scal_ref[2 + tb]
        last = scal_ref[2 + blocks + tb]

        def tile(jb, masked):
            j0 = jb * JB
            if masked:
                keep = []
                zero = jnp.zeros((SUB, LANES), jnp.bfloat16)
                one = jnp.ones((SUB, LANES), jnp.bfloat16)
                for inner in range(JB):
                    at = jnp.full((SUB, LANES), (j0 + inner).astype(jnp.float32)).astype(jnp.bfloat16)
                    keep.append(
                        [jnp.minimum(jnp.maximum(r_ref[t0 + i] - at, zero), one) for i in range(TB)]
                    )
            for g in range(groups):
                u = [u_ref[g, t0 + i] for i in range(TB)]
                products = [[] for _ in range(TB)]
                for inner in range(JB):
                    tap = j0 + inner
                    base = t0 + span * tap
                    x = [x_ref[g, base + i] for i in range(TB)]
                    if masked:
                        x = [a * m for a, m in zip(x, keep[inner])]
                    f = f4_ref[g, tap]
                    for i in range(TB):
                        products[i].append(f * x[i])
                    cols_ref[g, tap] += tree([u[i] * x[i] for i in range(TB)]).astype(jnp.float32)
                for i in range(TB):
                    total_ref[g, t0 + i] += tree(products[i]).astype(jnp.float32)

        def fast_step(jb, c):
            tile(jb, False)
            return c

        def slow_step(jb, c):
            tile(jb, True)
            return c

        lax.fori_loop(0, fast, fast_step, 0)
        lax.fori_loop(fast, last, slow_step, 0)
        for g in range(groups):
            for i in range(TB):
                side_ref[g, pl.ds(t0 + i, SUB, stride=length), :] = total_ref[g, t0 + i]
        return 0

    lax.fori_loop(0, blocks, token_block, 0)
    for g in range(groups):
        lanes = slice(g * LANES, (g + 1) * LANES)
        gi_ref[lanes, :] = side_ref[g].T.astype(jnp.bfloat16)
        gf_ref[lanes, :] = jnp.sum(cols_ref[g], axis=1).T * scale


def shifted(block, axis, distance):
    devices = range(lax.axis_size(axis))
    route = [(i - distance, i) for i in devices if i - distance in devices]
    return lax.ppermute(block, axis, route)


def on_device(
    cotangent, out_weight, gate_act, conv_input, conv_output, filters, dilation, segment_ids
):
    channels, rows = gate_act.shape
    ctx_count = lax.axis_size("ctx")
    position = lax.axis_index("ctx")
    tokens = rows * ctx_count
    longest = tokens // 2
    groups = channels // LANES
    length = rows // SUB
    reach = min(MAXDIL * KT, longest)
    depth = min(ctx_count - 1, (reach + rows - 1) // rows)

    grad_mix = lax.dot_general(
        out_weight, cotangent, (((1,), (1,)), ((), ())), preferred_element_type=jnp.float32
    )
    grad_gate = (grad_mix * conv_output.astype(jnp.float32)).astype(jnp.bfloat16)
    carried = (grad_mix * gate_act.astype(jnp.float32)).astype(jnp.bfloat16)
    pieces = [carried] + [shifted(carried, "ctx", -k) for k in range(1, depth + 1)]
    need = max(rows + reach, rows * (depth + 1))
    span = dilation[0]
    ends = jnp.sum(
        (segment_ids[None, :] <= jnp.arange(NDOCS, dtype=jnp.int32)[:, None]).astype(jnp.int32), axis=1
    )
    mine = lax.dynamic_slice_in_dim(segment_ids, position * rows, rows, 0)
    end = jnp.zeros((rows,), jnp.int32)
    for doc in range(NDOCS):
        end = jnp.where(mine == doc, ends[doc], end)
    at = position * rows + jnp.arange(rows, dtype=jnp.int32)
    room = jnp.minimum((end - at + span - 1) // span, KT).reshape(SUB, length)
    per = room.reshape(SUB, length // TB, TB)
    fast = jnp.min(per, axis=(0, 2)) // JB
    last = (jnp.max(per, axis=(0, 2)) + JB - 1) // JB
    built = jnp.minimum(length + span * JB * jnp.max(last), length + reach) // TB
    scal = jnp.concatenate([span[None], built[None], fast, last]).astype(jnp.int32)
    r4 = jnp.broadcast_to(room.T.astype(jnp.bfloat16)[:, :, None], (length, SUB, LANES))

    whole = pl.BlockSpec(memory_space=pltpu.VMEM)
    f32, bf16 = jnp.float32, jnp.bfloat16
    grad_input, cols = pl.pallas_call(
        functools.partial(conv_kernel, scale=1.0 / math.sqrt(tokens)),
        out_shape=(
            jax.ShapeDtypeStruct((channels, rows), bf16),
            jax.ShapeDtypeStruct((channels, KT), f32),
        ),
        in_specs=[pl.BlockSpec(memory_space=pltpu.SMEM)] + [whole] * (3 + len(pieces)),
        out_specs=(whole, whole),
        scratch_shapes=[
            pltpu.VMEM((groups, need, LANES), f32),
            pltpu.VMEM((groups, length, need // length, LANES), f32),
            pltpu.VMEM((groups, rows, LANES), f32),
            pltpu.VMEM((groups, length + reach, SUB, LANES), bf16),
            pltpu.VMEM((groups, length, SUB, LANES), bf16),
            pltpu.VMEM((groups, KT, SUB, LANES), bf16),
            pltpu.VMEM((groups, length, SUB, LANES), f32),
            pltpu.VMEM((groups, KT, SUB, LANES), f32),
        ],
        compiler_params=pltpu.CompilerParams(vmem_limit_bytes=56 * 1024 * 1024),
    )(scal, conv_input, r4, filters.T, *pieces)

    def partner(step):
        return [(i, i ^ step) for i in range(ctx_count)]

    half = channels // 2
    odd = position % 2
    mine = lax.dynamic_slice_in_dim(cols, odd * half, half, 0)
    away = lax.dynamic_slice_in_dim(cols, (1 - odd) * half, half, 0)
    mine = mine + lax.ppermute(away, "ctx", partner(1))
    step = 2
    while step < ctx_count:
        mine = mine + lax.ppermute(mine, "ctx", partner(step))
        step *= 2
    away = lax.ppermute(mine, "ctx", partner(1))
    first = jnp.where(odd == 0, mine, away)
    second = jnp.where(odd == 0, away, mine)
    cols = jnp.concatenate([first, second], axis=0)
    return (grad_gate, grad_input, cols)


def solution(mesh):
    in_specs = (
        P("ctx", None),
        P("ch", None),
        P("ch", "ctx"),
        P("ch", "ctx"),
        P("ch", "ctx"),
        P("ch", None),
        P("ch"),
        P(),
    )
    out_specs = (P("ch", "ctx"), P("ch", "ctx"), P("ch", None))
    return jax.shard_map(
        on_device, mesh=mesh, in_specs=in_specs, out_specs=out_specs, check_vma=False
    )
```
